1024 devices in a mesh: ctx: 64 (over x_hi, z), head: 16 (over y, x_lo, core).
Axes of the slice: x: 4 (x_hi: 2, x_lo: 2; x = x_hi * 2 + x_lo), y: 4, z: 32, core: 2. Of those that a mesh axis runs over, the one named last changes fastest.
Arguments:
- query_rows: bfloat16 [12288, 4096], P('ctx', 'head'), may hold values from -4.5 to 4.5
- key_rows: bfloat16 [12288, 512], P('ctx'), may hold values from -4.5 to 4.5
- value_rows: bfloat16 [12288, 512], P('ctx'), may hold values from -6 to 6
- w_out: bfloat16 [4096, 2048], P('head'), may hold values from -0.09375 to 0.09375
Outputs:
- mixed: bfloat16 [12288, 2048], P('ctx', 'head')
The draws below stay inside these ranges and needn't reach their ends.
All inputs are finite; a program needn't handle non-finite values.
Results may differ from the reference program's by a relative error of at most 0.019.
Values may be sent and summed in bfloat16 or wider, within the bound.
A program may use at most 32 MiB of HBM per device.

```python
import math
import jax
import jax.numpy as jnp
from jax import lax

D = 2048
HQ = 32
KVH = 4
HD = 128
TOK_DEV = 192
TOKENS = 12288


clip_bound = 4.5


def draw_query_rows(key, part):
    sample = jax.random.normal(jax.random.fold_in(key, 1), (TOKENS, HQ * HD), jnp.float32)
    return jnp.clip(sample, -clip_bound, clip_bound).astype(jnp.bfloat16)


def draw_key_rows(key, part):
    sample = jax.random.normal(jax.random.fold_in(key, 2), (TOKENS, KVH * HD), jnp.float32)
    return jnp.clip(sample, -clip_bound, clip_bound).astype(jnp.bfloat16)


def level_of(key, dims, pieces, smallest, largest):
    def one(axis_at, shards_of):
        heights = jax.random.uniform(jax.random.fold_in(jax.random.fold_in(key, 6), axis_at), (shards_of,), jnp.float32, smallest / len(pieces), largest / len(pieces))
        return jnp.repeat(jnp.exp(heights), dims[axis_at] // shards_of).reshape((-1,) + (1,) * (len(dims) - axis_at - 1))

    gain = one(*pieces[0])
    for cut in pieces[1:]:
        gain = gain * one(*cut)
    return gain


def centred(stream_key, dims, scale, bound, pieces=(), kind=jnp.bfloat16):
    result = jax.random.normal(stream_key, dims, jnp.float32) * scale
    if len(pieces) > 0:
        result = level_of(stream_key, dims, pieces, -0.22, 0.18) * result
    return jnp.clip(result, min=-bound, max=bound).astype(kind)


def setup_inputs(seed: int = 0) -> dict:
    splits = jax.random.split(jax.random.key(seed), 5)
    query_rows = draw_query_rows(jax.random.fold_in(splits[4], 71), 0)
    key_rows = draw_key_rows(jax.random.fold_in(splits[4], 71), 0)
    value_rows = centred(splits[2], (TOKENS, KVH * HD), 1.0, 6.0, ((0, 64),))
    w_out = centred(splits[3], (HQ * HD, D), (HQ * HD) ** -0.5, 0.09375, ((0, 16),))
    return {"query_rows": query_rows, "key_rows": key_rows, "value_rows": value_rows, "w_out": w_out}


def reference(query_rows, key_rows, value_rows, w_out):
    tokens_all = query_rows.shape[0]
    group_size = HQ // KVH
    score_scale = 1.0 / math.sqrt(HD)
    grouped = query_rows.reshape(tokens_all, KVH, group_size, HD)
    key_heads = key_rows.astype(jnp.float32).reshape(tokens_all, KVH, HD)
    value_heads = value_rows.astype(jnp.float32).reshape(tokens_all, KVH, HD)
    key_positions = jnp.arange(tokens_all, dtype=jnp.int32)

    def one_block(block_number):
        first_row = block_number * TOK_DEV
        block_queries = lax.dynamic_slice_in_dim(grouped, first_row, TOK_DEV, 0).astype(jnp.float32)
        scores = jnp.einsum('tgjd,sgd->gjts', block_queries, key_heads) * score_scale
        query_positions = first_row + jnp.arange(TOK_DEV, dtype=jnp.int32)
        allowed = key_positions[None, :] <= query_positions[:, None]
        scores = jnp.where(allowed, scores, -1e+30)
        maximum = lax.optimization_barrier(jnp.max(scores, axis=3, keepdims=True))
        raised = jnp.where(allowed, jnp.exp(scores - maximum), 0.0)
        denominator = lax.optimization_barrier(jnp.sum(raised, axis=3))
        rounded = lax.optimization_barrier(raised.astype(jnp.bfloat16))
        weights = rounded.astype(jnp.float32)
        numerator = jnp.einsum('gjts,sgd->tgjd', weights, value_heads)
        scaled = numerator / jnp.transpose(denominator, (2, 0, 1))[:, :, :, None]
        return scaled.astype(jnp.bfloat16).reshape(TOK_DEV, HQ * HD)
    blocks = lax.map(one_block, jnp.arange(tokens_all // TOK_DEV, dtype=jnp.int32))
    attended = blocks.reshape(tokens_all, HQ * HD)
    return jnp.dot(attended, w_out, preferred_element_type=jnp.float32).astype(jnp.bfloat16)
```

```python
import math

import jax
import jax.numpy as jnp
from jax import lax
from jax.experimental import pallas as pl
from jax.experimental.pallas import tpu as pltpu
from jax.sharding import PartitionSpec as P

MESH = pl.DeviceIdType.MESH
HD = 128
RING = 32
TOK = 192
ROWS = 96
PIECE = 48
COLS = 4 * ROWS
FLOOR = -1e20
MASKED = -1e30
EXP2 = math.log2(math.e) / math.sqrt(HD)

OFFSET = {0: 0, 1: 1, 3: -1, 2: 2}
WAVES = [
    [(0, 0), (1, 0), (3, 0), (2, 0), (2, 7)],
    [(0, 1), (0, 7), (1, 1), (1, 7), (3, 1), (3, 7), (2, 1), (2, 6)],
    [(0, 2), (0, 6), (1, 2), (1, 6), (3, 2), (3, 6), (2, 2), (2, 5)],
    [(0, 3), (0, 5), (1, 3), (1, 5), (3, 3), (3, 5), (2, 3), (2, 4)],
    [(0, 4), (1, 4), (3, 4)],
]
ORDER = [chunk for wave in WAVES for chunk in wave]
PLACE = {chunk: place for place, chunk in enumerate(ORDER)}
SHIFT = [(OFFSET[g] + 4 * j) % RING for g, j in ORDER]
CHAIN = {0: [(4, (0, 7)), (-4, (0, 1))], 7: [(4, (0, 6))], 6: [(4, (0, 5))], 1: [(-4, (0, 2))], 2: [(-4, (0, 3))]}


def near(slot):
    steps = [(1, (3, slot)), (-1, (1, slot))]
    if slot in (0, 7, 6, 5):
        steps.append((2, (2, (slot - 1) % 8)))
    if slot in (0, 1, 2, 3):
        steps.append((-2, (2, slot)))
    return steps


def kernel(
    q_in, k_in, v_in, w_in, out,
    kv, q, w, acc, stats, sent, got, got_stats, parts, landed,
    load_sem, z_send, z_recv, last_send, pair_send, pair_recv, q_send, q_recv, w_send, w_recv,
    merge_send, merge_recv, sum_send, sum_recv,
):
    ctx, head = lax.axis_index("ctx"), lax.axis_index("head")
    x_hi, z = lax.div(ctx, RING), lax.rem(ctx, RING)
    y, x_lo, core = lax.div(head, 4), lax.rem(lax.div(head, 2), 2), lax.rem(head, 2)
    other = 1 - core
    pair = lax.div(head, 2)

    def along_z(step):
        return (x_hi * RING + lax.rem(z + step + RING, RING), head)

    def along_x(xi, kd):
        hi = 1 - x_hi if xi & 2 else x_hi
        lo = 1 - x_lo if xi & 1 else x_lo
        return (hi * RING + z, y * 4 + lo * 2 + kd)

    def in_slice(i2, kd):
        lo = 1 - x_lo if i2 & 1 else x_lo
        yy = y
        if i2 & 2:
            yy = yy + 1 - 2 * lax.rem(y, 2)
        if i2 & 4:
            yy = lax.rem(yy + 2, 4)
        return (ctx, yy * 4 + lo * 2 + kd)

    def remote(src, dst, send, recv, device):
        return pltpu.make_async_remote_copy(
            src_ref=src, dst_ref=dst, send_sem=send, recv_sem=recv, device_id=device, device_id_type=MESH
        )

    first = pl.multiple_of(x_lo * ROWS + core * PIECE, 16)
    column = pl.multiple_of(y * HD, HD)
    own_k = pltpu.make_async_copy(
        k_in.at[pl.ds(first, PIECE), pl.ds(column, HD)], kv.at[core, 0, :, pl.ds(0, HD)], load_sem.at[0]
    )
    own_v = pltpu.make_async_copy(
        v_in.at[pl.ds(first, PIECE), pl.ds(column, HD)], kv.at[core, 0, :, pl.ds(HD, HD)], load_sem.at[1]
    )
    own_q = pltpu.make_async_copy(
        q_in.at[pl.ds(pl.multiple_of(core * ROWS, 16), ROWS)], q.at[0, core], load_sem.at[2]
    )
    own_w = pltpu.make_async_copy(w_in, w.at[core], load_sem.at[3])
    own_k.start()
    own_v.start()
    own_q.start()
    own_w.start()

    barrier = pltpu.get_barrier_semaphore()
    peers = [along_z(step) for step in (4, -4, 2, -2, 1, -1)]
    peers += [along_x(xi, kd) for xi in (2, 3) for kd in (core, other)]
    peers += [in_slice(i2, kd) for i2 in range(8) for kd in (core, other) if (i2, kd is core) != (0, True)]
    for peer in peers:
        pl.semaphore_signal(barrier, inc=1, device_id=peer, device_id_type=MESH)
    acc[...] = jnp.zeros_like(acc)
    row = lax.broadcasted_iota(jnp.int32, stats.shape, 1)
    stats[...] = jnp.where(row == 0, FLOOR, 0.0).astype(jnp.float32)
    own_k.wait()
    own_v.wait()
    pl.semaphore_wait(barrier, len(peers))

    waiting = []

    def z_copy(slot, step, chunk):
        place = PLACE[chunk]
        return remote(
            kv.at[core, PLACE[(0, slot)]], kv.at[core, place], z_send.at[place], z_recv.at[place], along_z(step)
        )

    def pass_on(slot):
        for step, chunk in CHAIN.get(slot, []) + near(slot):
            copy = z_copy(slot, step, chunk)
            copy.start()
            waiting.append(copy)

    def arrived(chunk):
        place = PLACE[chunk]
        remote(
            kv.at[core, place], kv.at[core, place], z_send.at[place], z_recv.at[place], along_z(4)
        ).wait_recv()

    pass_on(0)

    q_copies = []
    for xi in (2, 3, 1, 0):
        for same in (True, False):
            if (xi, same) == (0, True):
                continue
            kd = core if same else other
            copy = remote(
                q_in.at[pl.ds(pl.multiple_of(kd * ROWS, 16), ROWS)],
                q.at[xi, core],
                q_send.at[xi, int(same)],
                q_recv.at[xi, int(same)],
                along_x(xi, kd),
            )
            copy.start()
            q_copies.append((xi, same, copy))
            waiting.append(copy)
    w_copy = remote(w_in, w.at[core], w_send, w_recv, in_slice(0, other))
    w_copy.start()
    waiting.append(w_copy)

    def exchange(wave):
        begin, count = PLACE[WAVES[wave][0]], len(WAVES[wave])
        piece = kv.at[core, pl.ds(begin, count)]
        copy = remote(piece, piece, pair_send.at[wave], pair_recv.at[wave], in_slice(0, other))
        copy.start()
        waiting.append(copy)
        theirs = kv.at[other, pl.ds(begin, count)]
        remote(theirs, theirs, pair_send.at[wave], pair_recv.at[wave], in_slice(0, other)).wait_recv()

    def attend(wave, xi, masked):
        begin, count = PLACE[WAVES[wave][0]], len(WAVES[wave])
        queries = jnp.concatenate(
            [q[xi, ks, :, e * HD : (e + 1) * HD] for ks in range(2) for e in range(2)], axis=0
        )
        scores, values = [], []
        for half in range(2):
            block = kv[half, begin : begin + count].reshape(count * PIECE, 2 * HD)
            s = lax.dot_general(
                block[:, :HD], queries, (((1,), (1,)), ((), ())), preferred_element_type=jnp.float32
            )
            if masked:
                pieces = []
                for n in range(count):
                    part = s[n * PIECE : (n + 1) * PIECE]
                    shift = SHIFT[begin + n]
                    if shift == 0:
                        key = lax.broadcasted_iota(jnp.int32, part.shape, 0) + (x_lo * ROWS + half * PIECE)
                        query = lax.rem(lax.broadcasted_iota(jnp.int32, part.shape, 1), ROWS) + core * ROWS
                        pieces.append(jnp.where(key <= query, part, MASKED))
                    else:
                        allowed = lax.rem(z + shift, RING) < z
                        pieces.append(part + jnp.where(allowed, 0.0, MASKED).astype(jnp.float32))
                s = jnp.concatenate(pieces, axis=0)
            scores.append(s)
            values.append(block[:, HD:])
        old = stats[xi, 0:1, :]
        top = old
        for s in scores:
            top = jnp.maximum(top, jnp.max(s, axis=0, keepdims=True))
        factor = jnp.exp2((old - top) * EXP2)
        total = stats[xi, 1:2, :] * factor
        result = acc[xi] * factor
        for s, v in zip(scores, values):
            p = jnp.exp2((s - top) * EXP2)
            total += jnp.sum(p, axis=0, keepdims=True)
            result += lax.dot_general(
                v, p.astype(jnp.bfloat16), (((0,), (0,)), ((), ())), preferred_element_type=jnp.float32
            )
        acc[xi] = result
        stats[xi, 0:1, :] = top
        stats[xi, 1:2, :] = total

    def attend_all(wave):
        @pl.when(x_hi == 0)
        def _():
            @pl.loop(2, 4)
            def _(xi):
                attend(wave, xi, False)

        @pl.loop(0, 2)
        def _(xi):
            attend(wave, xi, True)

    for wave in range(len(WAVES)):
        if wave + 1 < len(WAVES):
            for chunk in WAVES[wave + 1]:
                if chunk[0] == 0:
                    arrived(chunk)
                    if chunk[1] in (5, 3):
                        continue
                    pass_on(chunk[1])
            if wave == 2:
                last = remote(
                    kv.at[core, PLACE[(0, 3)] + other],
                    kv.at[core, PLACE[(0, 4)]],
                    last_send,
                    z_recv.at[PLACE[(0, 4)]],
                    (x_hi * RING + lax.rem(z + 4 - 8 * core + RING, RING), head),
                )
                last.start()
                waiting.append(last)
                pass_on(3)
                pass_on(5)
        for chunk in WAVES[wave]:
            if chunk[0] != 0:
                arrived(chunk)
        exchange(wave)
        if wave == 0:
            own_q.wait()
            for xi, same, copy in q_copies:
                ks = core if same else other
                remote(
                    q.at[xi, ks], q.at[xi, ks], q_send.at[xi, int(same)], q_recv.at[xi, int(same)], along_x(xi, ks)
                ).wait_recv()
        attend_all(wave)

    def give(xi):
        sent[xi] = acc[xi].astype(jnp.bfloat16)
        return [
            remote(sent.at[xi], got.at[xi], merge_send.at[xi, 0], merge_recv.at[xi, 0], along_x(xi, core)),
            remote(stats.at[xi], got_stats.at[xi], merge_send.at[xi, 1], merge_recv.at[xi, 1], along_x(xi, core)),
        ]

    def take(xi):
        return [
            remote(got.at[xi], got.at[xi], merge_send.at[xi, 0], merge_recv.at[xi, 0], along_x(xi, core)),
            remote(got_stats.at[xi], got_stats.at[xi], merge_send.at[xi, 1], merge_recv.at[xi, 1], along_x(xi, core)),
        ]

    for xi in (2, 3, 1):
        for copy in give(xi):
            copy.start()
            waiting.append(copy)
    for xi in (1, 3, 2):
        for copy in take(xi):
            copy.wait_recv()

    tops = [stats[0, 0:1, :]] + [got_stats[xi, 0:1, :] for xi in (1, 2, 3)]
    top = jnp.maximum(jnp.maximum(tops[0], tops[1]), jnp.maximum(tops[2], tops[3]))
    factors = [jnp.exp2((t - top) * EXP2) for t in tops]
    total = stats[0, 1:2, :] * factors[0]
    result = acc[0] * factors[0]
    for xi in (1, 2, 3):
        total += got_stats[xi, 1:2, :] * factors[xi]
        result += got[xi].astype(jnp.float32) * factors[xi]
    turned = jnp.transpose(result / total).astype(jnp.bfloat16)
    attended = jnp.concatenate([turned[n * ROWS : (n + 1) * ROWS] for n in range(4)], axis=1)

    own_w.wait()
    remote(w_in, w.at[other], w_send, w_recv, in_slice(0, other)).wait_recv()
    for i2 in (6, 7, 4, 5, 2, 3, 1, 0):
        chip = in_slice(i2, 0)[1]
        columns = pl.ds(pl.multiple_of(chip * HD, 2 * HD), 2 * HD)
        sums = jnp.dot(attended[:, : 2 * HD], w[0, :, columns], preferred_element_type=jnp.float32)
        sums += jnp.dot(attended[:, 2 * HD :], w[1, :, columns], preferred_element_type=jnp.float32)
        for kd in range(2):
            parts[i2, kd] = sums[:, kd * HD : (kd + 1) * HD].astype(jnp.bfloat16)
        if i2:
            for kd in range(2):
                copy = remote(
                    parts.at[i2, kd],
                    landed.at[i2, core],
                    sum_send.at[i2, kd],
                    sum_recv.at[i2, core],
                    in_slice(i2, kd),
                )
                copy.start()
                waiting.append(copy)
        else:
            copy = remote(
                parts.at[0, other],
                landed.at[0, core],
                sum_send.at[0, 0],
                sum_recv.at[0, core],
                in_slice(0, other),
            )
            copy.start()
            waiting.append(copy)
    landed[0, core] = parts[0, core]
    for i2 in range(8):
        for ks in range(2) if i2 else (other,):
            remote(
                landed.at[i2, ks], landed.at[i2, ks], sum_send.at[i2, 0], sum_recv.at[i2, ks], in_slice(i2, other)
            ).wait_recv()
    for ks in range(2):
        sums = landed[0, ks].astype(jnp.float32)
        for i2 in range(1, 8):
            sums += landed[i2, ks].astype(jnp.float32)
        out[ks * ROWS : (ks + 1) * ROWS] = sums.astype(jnp.bfloat16)
    for copy in waiting:
        copy.wait_send()


def on_device(query_rows, key_rows, value_rows, w_out):
    bf16, f32 = jnp.bfloat16, jnp.float32
    dma = pltpu.SemaphoreType.DMA
    chunks = len(ORDER)
    return pl.pallas_call(
        kernel,
        out_shape=jax.ShapeDtypeStruct((TOK, HD), bf16),
        in_specs=[pl.BlockSpec(memory_space=pl.ANY)] * 4,
        out_specs=pl.BlockSpec(memory_space=pltpu.VMEM),
        scratch_shapes=[
            pltpu.VMEM((2, chunks, PIECE, 2 * HD), bf16),
            pltpu.VMEM((4, 2, ROWS, 2 * HD), bf16),
            pltpu.VMEM((2,) + w_out.shape, bf16),
            pltpu.VMEM((4, HD, COLS), f32),
            pltpu.VMEM((4, 8, COLS), f32),
            pltpu.VMEM((4, HD, COLS), bf16),
            pltpu.VMEM((4, HD, COLS), bf16),
            pltpu.VMEM((4, 8, COLS), f32),
            pltpu.VMEM((8, 2, ROWS, HD), bf16),
            pltpu.VMEM((8, 2, ROWS, HD), bf16),
            dma((4,)),
            dma((chunks,)),
            dma((chunks,)),
            dma,
            dma((len(WAVES),)),
            dma((len(WAVES),)),
            dma((4, 2)),
            dma((4, 2)),
            dma,
            dma,
            dma((4, 2)),
            dma((4, 2)),
            dma((8, 2)),
            dma((8, 2)),
        ],
        compiler_params=pltpu.CompilerParams(
            collective_id=0, has_side_effects=True, vmem_limit_bytes=56 * 1024 * 1024
        ),
        name="attention",
    )(query_rows, key_rows, value_rows, w_out)


def solution(mesh):
    placed = (P("ctx", "head"), P("ctx", None), P("ctx", None), P("head", None))
    return jax.shard_map(
        on_device, mesh=mesh, in_specs=placed, out_specs=P("ctx", "head"), check_vma=False
    )
```

```python
import math

import jax
import jax.numpy as jnp
from jax import lax
from jax.experimental import pallas as pl
from jax.experimental.pallas import tpu as pltpu
from jax.sharding import PartitionSpec as P

MESH = pl.DeviceIdType.MESH
HD = 128
RING = 32
TOK = 192
ROWS = 96
PIECE = 48
COLS = 4 * ROWS
FLOOR = -1e20
MASKED = -1e30
EXP2 = math.log2(math.e) / math.sqrt(HD)

OFFSET = {0: 0, 1: 1, 3: -1, 2: 2}
WAVES = [
    [(0, 0), (1, 0), (3, 0), (2, 0), (2, 7)],
    [(0, 1), (0, 7), (1, 1), (1, 7), (3, 1), (3, 7), (2, 1), (2, 6)],
    [(0, 2), (0, 6), (1, 2), (1, 6), (3, 2), (3, 6), (2, 2), (2, 5)],
    [(0, 3), (0, 5), (1, 3), (1, 5), (3, 3), (3, 5)],
    [(2, 3), (2, 4), (1, 4), (3, 4), (0, 4)],
]
ORDER = [chunk for wave in WAVES for chunk in wave]
PLACE = {chunk: place for place, chunk in enumerate(ORDER)}
SHIFT = [(OFFSET[g] + 4 * j) % RING for g, j in ORDER]
CHAIN = {0: [(4, (0, 7)), (-4, (0, 1))], 7: [(4, (0, 6))], 6: [(4, (0, 5))], 1: [(-4, (0, 2))], 2: [(-4, (0, 3))]}


def near(slot):
    if slot == 4:
        return []
    steps = [(1, (3, slot)), (-1, (1, slot))]
    if slot == 5:
        steps.append((3, (1, 4)))
    if slot == 3:
        steps.append((-3, (3, 4)))
    if slot in (0, 7, 6, 5):
        steps.append((2, (2, (slot - 1) % 8)))
    if slot in (0, 1, 2, 3):
        steps.append((-2, (2, slot)))
    return steps


def kernel(
    q_in, k_in, v_in, w_in, landed,
    kv, q, w, acc, stats, sent, got, got_stats, parts,
    load_sem, z_send, z_recv, last_send, pair_send, pair_recv, q_send, q_recv, w_send, w_recv,
    merge_send, merge_recv, sum_send, sum_recv,
):
    ctx, head = lax.axis_index("ctx"), lax.axis_index("head")
    x_hi, z = lax.div(ctx, RING), lax.rem(ctx, RING)
    y, x_lo, core = lax.div(head, 4), lax.rem(lax.div(head, 2), 2), lax.rem(head, 2)
    other = 1 - core
    pair = lax.div(head, 2)

    def along_z(step):
        return (x_hi * RING + lax.rem(z + step + RING, RING), head)

    def along_x(xi, kd):
        hi = 1 - x_hi if xi & 2 else x_hi
        lo = 1 - x_lo if xi & 1 else x_lo
        return (hi * RING + z, y * 4 + lo * 2 + kd)

    def in_slice(i2, kd):
        lo = 1 - x_lo if i2 & 1 else x_lo
        yy = y
        if i2 & 2:
            yy = yy + 1 - 2 * lax.rem(y, 2)
        if i2 & 4:
            yy = lax.rem(yy + 2, 4)
        return (ctx, yy * 4 + lo * 2 + kd)

    def remote(src, dst, send, recv, device):
        return pltpu.make_async_remote_copy(
            src_ref=src, dst_ref=dst, send_sem=send, recv_sem=recv, device_id=device, device_id_type=MESH
        )

    first = pl.multiple_of(x_lo * ROWS + core * PIECE, 16)
    column = pl.multiple_of(y * HD, HD)
    own_k = pltpu.make_async_copy(
        k_in.at[pl.ds(first, PIECE), pl.ds(column, HD)], kv.at[core, 0, :, pl.ds(0, HD)], load_sem.at[0]
    )
    own_v = pltpu.make_async_copy(
        v_in.at[pl.ds(first, PIECE), pl.ds(column, HD)], kv.at[core, 0, :, pl.ds(HD, HD)], load_sem.at[1]
    )
    own_q = pltpu.make_async_copy(
        q_in.at[pl.ds(pl.multiple_of(core * ROWS, 16), ROWS)], q.at[0, core], load_sem.at[2]
    )
    own_w = pltpu.make_async_copy(w_in, w.at[core], load_sem.at[3])
    barrier = pltpu.get_barrier_semaphore()
    peers = [along_z(step) for step in (4, -4, 3, -3, 2, -2, 1, -1)]
    peers += [along_x(xi, kd) for xi in (2, 3) for kd in (core, other)]
    peers += [in_slice(i2, kd) for i2 in range(8) for kd in (core, other) if (i2, kd is core) != (0, True)]
    for peer in peers:
        pl.semaphore_signal(barrier, inc=1, device_id=peer, device_id_type=MESH)
    own_k.start()
    own_v.start()
    own_q.start()
    own_w.start()
    acc[...] = jnp.zeros_like(acc)
    row = lax.broadcasted_iota(jnp.int32, stats.shape, 1)
    stats[...] = jnp.where(row == 0, FLOOR, 0.0).astype(jnp.float32)
    own_k.wait()
    own_v.wait()
    pl.semaphore_wait(barrier, len(peers))

    waiting = []

    def z_copy(slot, step, chunk):
        place = PLACE[chunk]
        return remote(
            kv.at[core, PLACE[(0, slot)]], kv.at[core, place], z_send.at[place], z_recv.at[place], along_z(step)
        )

    def pass_on(slot):
        for step, chunk in CHAIN.get(slot, []) + near(slot):
            copy = z_copy(slot, step, chunk)
            copy.start()
            waiting.append(copy)

    def arrived(chunk):
        place = PLACE[chunk]
        remote(
            kv.at[core, place], kv.at[core, place], z_send.at[place], z_recv.at[place], along_z(4)
        ).wait_recv()

    pass_on(0)

    q_copies = []
    for xi in (2, 3, 1, 0):
        for same in (True, False):
            if (xi, same) == (0, True):
                continue
            kd = core if same else other
            copy = remote(
                q_in.at[pl.ds(pl.multiple_of(kd * ROWS, 16), ROWS)],
                q.at[xi, core],
                q_send.at[xi, int(same)],
                q_recv.at[xi, int(same)],
                along_x(xi, kd),
            )
            copy.start()
            q_copies.append((xi, same, copy))
            waiting.append(copy)
    w_copy = remote(w_in, w.at[core], w_send, w_recv, in_slice(0, other))
    w_copy.start()
    waiting.append(w_copy)

    def exchange(wave):
        begin, count = PLACE[WAVES[wave][0]], len(WAVES[wave])
        piece = kv.at[core, pl.ds(begin, count)]
        copy = remote(piece, piece, pair_send.at[wave], pair_recv.at[wave], in_slice(0, other))
        copy.start()
        waiting.append(copy)

    def exchanged(wave):
        begin, count = PLACE[WAVES[wave][0]], len(WAVES[wave])
        theirs = kv.at[other, pl.ds(begin, count)]
        remote(theirs, theirs, pair_send.at[wave], pair_recv.at[wave], in_slice(0, other)).wait_recv()

    def attend(wave, xi, masked):
        begin, count = PLACE[WAVES[wave][0]], len(WAVES[wave])
        queries = jnp.concatenate(
            [q[xi, ks, :, e * HD : (e + 1) * HD] for ks in range(2) for e in range(2)], axis=0
        )
        scores, values = [], []
        for half in range(2):
            block = kv[half, begin : begin + count].reshape(count * PIECE, 2 * HD)
            s = lax.dot_general(
                block[:, :HD], queries, (((1,), (1,)), ((), ())), preferred_element_type=jnp.float32
            )
            if masked:
                pieces = []
                for n in range(count):
                    part = s[n * PIECE : (n + 1) * PIECE]
                    shift = SHIFT[begin + n]
                    if shift == 0:
                        key = lax.broadcasted_iota(jnp.int32, part.shape, 0) + (x_lo * ROWS + half * PIECE)
                        query = lax.rem(lax.broadcasted_iota(jnp.int32, part.shape, 1), ROWS) + core * ROWS
                        pieces.append(jnp.where(key <= query, part, MASKED))
                    else:
                        allowed = lax.rem(z + shift, RING) < z
                        pieces.append(part + jnp.where(allowed, 0.0, MASKED).astype(jnp.float32))
                s = jnp.concatenate(pieces, axis=0)
            scores.append(s)
            values.append(block[:, HD:])
        old = stats[xi, 0:1, :]
        top = old
        for s in scores:
            top = jnp.maximum(top, jnp.max(s, axis=0, keepdims=True))
        factor = jnp.exp2((old - top) * EXP2)
        total = stats[xi, 1:2, :] * factor
        result = acc[xi] * factor
        for s, v in zip(scores, values):
            p = jnp.exp2((s - top) * EXP2)
            total += jnp.sum(p, axis=0, keepdims=True)
            result += lax.dot_general(
                v, p.astype(jnp.bfloat16), (((0,), (0,)), ((), ())), preferred_element_type=jnp.float32
            )
        acc[xi] = result
        stats[xi, 0:1, :] = top
        stats[xi, 1:2, :] = total

    def attend_all(wave):
        @pl.when(x_hi == 0)
        def _():
            @pl.loop(2, 4)
            def _(xi):
                attend(wave, xi, False)

        reached = wave == 0
        for place in range(PLACE[WAVES[wave][0]], PLACE[WAVES[wave][0]] + len(WAVES[wave])):
            if SHIFT[place]:
                reached |= lax.rem(z + SHIFT[place], RING) < z

        @pl.when(reached)
        def _():
            @pl.loop(0, 2)
            def _(xi):
                attend(wave, xi, True)

    for wave in range(len(WAVES)):
        if wave + 1 < len(WAVES):
            for chunk in WAVES[wave + 1]:
                if chunk[0] == 0 and chunk[1] != 4:
                    arrived(chunk)
                    if chunk[1] in (5, 3):
                        continue
                    pass_on(chunk[1])
            if wave == 2:
                last = remote(
                    kv.at[core, PLACE[(0, 3)] + other],
                    kv.at[core, PLACE[(0, 4)]],
                    last_send,
                    z_recv.at[PLACE[(0, 4)]],
                    (x_hi * RING + lax.rem(z + 4 - 8 * core + RING, RING), head),
                )
                last.start()
                waiting.append(last)
                pass_on(3)
                pass_on(5)
        for chunk in WAVES[wave]:
            if chunk[0] or chunk[1] == 4:
                arrived(chunk)
        exchange(wave)
        if wave == 0:
            own_q.wait()
            for xi, same, copy in q_copies:
                ks = core if same else other
                remote(
                    q.at[xi, ks], q.at[xi, ks], q_send.at[xi, int(same)], q_recv.at[xi, int(same)], along_x(xi, ks)
                ).wait_recv()
        else:
            exchanged(wave - 1)
            attend_all(wave - 1)
    exchanged(len(WAVES) - 1)
    attend_all(len(WAVES) - 1)

    def give(xi, wanted):
        @pl.when(wanted)
        def _():
            sent[xi] = acc[xi].astype(jnp.bfloat16)

        return [
            remote(sent.at[xi], got.at[xi], merge_send.at[xi, 0], merge_recv.at[xi, 0], along_x(xi, core)),
            remote(stats.at[xi], got_stats.at[xi], merge_send.at[xi, 1], merge_recv.at[xi, 1], along_x(xi, core)),
        ]

    def take(xi):
        return [
            remote(got.at[xi], got.at[xi], merge_send.at[xi, 0], merge_recv.at[xi, 0], along_x(xi, core)),
            remote(got_stats.at[xi], got_stats.at[xi], merge_send.at[xi, 1], merge_recv.at[xi, 1], along_x(xi, core)),
        ]

    from_low = [copy for xi in (2, 3) for copy in give(xi, x_hi == 0)]
    pl.when(x_hi == 0)(lambda: [copy.start() for copy in from_low] and None)
    for copy in give(1, True):
        copy.start()
        waiting.append(copy)

    def absorb(xi):
        for copy in take(xi):
            copy.wait_recv()
        mine, theirs = stats[0, 0:1, :], got_stats[xi, 0:1, :]
        top = jnp.maximum(mine, theirs)
        mine, theirs = jnp.exp2((mine - top) * EXP2), jnp.exp2((theirs - top) * EXP2)
        acc[0] = acc[0] * mine + got[xi].astype(jnp.float32) * theirs
        stats[0, 1:2, :] = stats[0, 1:2, :] * mine + got_stats[xi, 1:2, :] * theirs
        stats[0, 0:1, :] = top

    absorb(1)

    @pl.when(x_hi == 1)
    def _():
        absorb(3)
        absorb(2)

    turned = jnp.transpose(acc[0] / stats[0, 1:2, :]).astype(jnp.bfloat16)
    attended = jnp.concatenate([turned[n * ROWS : (n + 1) * ROWS] for n in range(4)], axis=1)

    own_w.wait()
    remote(w_in, w.at[other], w_send, w_recv, in_slice(0, other)).wait_recv()
    for i2 in (6, 7, 4, 5, 2, 3, 1, 0):
        chip = in_slice(i2, 0)[1]
        columns = pl.ds(pl.multiple_of(chip * HD, 2 * HD), 2 * HD)
        sums = jnp.dot(attended[:, : 2 * HD], w[0, :, columns], preferred_element_type=jnp.float32)
        sums += jnp.dot(attended[:, 2 * HD :], w[1, :, columns], preferred_element_type=jnp.float32)
        for kd in range(2):
            parts[i2, kd] = sums[:, kd * HD : (kd + 1) * HD].astype(jnp.bfloat16)
        if i2:
            for kd in range(2):
                copy = remote(
                    parts.at[i2, kd],
                    landed.at[i2, core],
                    sum_send.at[i2, kd],
                    sum_recv.at[i2, core],
                    in_slice(i2, kd),
                )
                copy.start()
                waiting.append(copy)
        else:
            copy = remote(
                parts.at[0, other],
                landed.at[0, core],
                sum_send.at[0, 0],
                sum_recv.at[0, core],
                in_slice(0, other),
            )
            copy.start()
            waiting.append(copy)
    keep = pltpu.make_async_copy(parts.at[0, core], landed.at[0, core], load_sem.at[4])
    keep.start()
    for i2 in range(8):
        for ks in range(2) if i2 else (other,):
            remote(
                landed.at[i2, ks], landed.at[i2, ks], sum_send.at[i2, 0], sum_recv.at[i2, ks], in_slice(i2, other)
            ).wait_recv()
    keep.wait()
    for copy in waiting:
        copy.wait_send()
    pl.when(x_hi == 0)(lambda: [copy.wait_send() for copy in from_low] and None)


def on_device(query_rows, key_rows, value_rows, w_out):
    bf16, f32 = jnp.bfloat16, jnp.float32
    dma = pltpu.SemaphoreType.DMA
    chunks = len(ORDER)
    landed = pl.pallas_call(
        kernel,
        out_shape=jax.ShapeDtypeStruct((8, 2, ROWS, HD), bf16),
        in_specs=[pl.BlockSpec(memory_space=pl.ANY)] * 4,
        out_specs=pl.BlockSpec(memory_space=pl.ANY),
        scratch_shapes=[
            pltpu.VMEM((2, chunks, PIECE, 2 * HD), bf16),
            pltpu.VMEM((4, 2, ROWS, 2 * HD), bf16),
            pltpu.VMEM((2,) + w_out.shape, bf16),
            pltpu.VMEM((4, HD, COLS), f32),
            pltpu.VMEM((4, 8, COLS), f32),
            pltpu.VMEM((4, HD, COLS), bf16),
            pltpu.VMEM((4, HD, COLS), bf16),
            pltpu.VMEM((4, 8, COLS), f32),
            pltpu.VMEM((8, 2, ROWS, HD), bf16),
            dma((5,)),
            dma((chunks,)),
            dma((chunks,)),
            dma,
            dma((len(WAVES),)),
            dma((len(WAVES),)),
            dma((4, 2)),
            dma((4, 2)),
            dma,
            dma,
            dma((4, 2)),
            dma((4, 2)),
            dma((8, 2)),
            dma((8, 2)),
        ],
        compiler_params=pltpu.CompilerParams(
            collective_id=0, has_side_effects=True, vmem_limit_bytes=56 * 1024 * 1024
        ),
        name="attention",
    )(query_rows, key_rows, value_rows, w_out)
    return jnp.sum(landed.astype(f32), axis=0).astype(bf16).reshape(TOK, HD)


def solution(mesh):
    placed = (P("ctx", "head"), P("ctx", None), P("ctx", None), P("head", None))
    return jax.shard_map(
        on_device, mesh=mesh, in_specs=placed, out_specs=P("ctx", "head"), check_vma=False
    )
```

```python
import math

import jax
import jax.numpy as jnp
from jax import lax
from jax.experimental import pallas as pl
from jax.experimental.pallas import tpu as pltpu
from jax.sharding import PartitionSpec as P

MESH = pl.DeviceIdType.MESH
HD = 128
RING = 32
TOK = 192
ROWS = 96
PIECE = 48
COLS = 4 * ROWS
FLOOR = -1e20
MASKED = -1e30
EXP2 = math.log2(math.e) / math.sqrt(HD)

OFFSET = {0: 0, 1: 1, 3: -1, 2: 2}
WAVES = [
    [(0, 0), (1, 0), (3, 0), (2, 0), (2, 7)],
    [(0, 1), (0, 7), (1, 1), (1, 7), (3, 1), (3, 7), (2, 1), (2, 6)],
    [(0, 2), (0, 6), (1, 2), (1, 6), (3, 2), (3, 6), (2, 2), (2, 5)],
    [(0, 3), (0, 5), (1, 3), (1, 5), (3, 3), (3, 5)],
    [(2, 3), (2, 4), (1, 4), (3, 4), (0, 4)],
]
ORDER = [chunk for wave in WAVES for chunk in wave]
PLACE = {chunk: place for place, chunk in enumerate(ORDER)}
SHIFT = [(OFFSET[g] + 4 * j) % RING for g, j in ORDER]
CHAIN = {0: [(4, (0, 7)), (-4, (0, 1))], 7: [(4, (0, 6))], 6: [(4, (0, 5))], 1: [(-4, (0, 2))], 2: [(-4, (0, 3))]}


def near(slot):
    if slot == 4:
        return []
    steps = [(1, (3, slot)), (-1, (1, slot))]
    if slot == 5:
        steps.append((3, (1, 4)))
    if slot == 3:
        steps.append((-3, (3, 4)))
    if slot in (0, 7, 6, 5):
        steps.append((2, (2, (slot - 1) % 8)))
    if slot in (0, 1, 2, 3):
        steps.append((-2, (2, slot)))
    return steps


def kernel(
    q_in, k_in, v_in, w_in, landed,
    kv, q, w, acc, stats, sent, got, got_stats, parts,
    load_sem, z_send, z_recv, last_send, pair_send, pair_recv, q_send, q_recv, w_send, w_recv,
    merge_send, merge_recv, sum_send, sum_recv,
):
    ctx, head = lax.axis_index("ctx"), lax.axis_index("head")
    x_hi, z = lax.div(ctx, RING), lax.rem(ctx, RING)
    y, x_lo, core = lax.div(head, 4), lax.rem(lax.div(head, 2), 2), lax.rem(head, 2)
    other = 1 - core
    pair = lax.div(head, 2)

    def along_z(step):
        return (x_hi * RING + lax.rem(z + step + RING, RING), head)

    def along_x(xi, kd):
        hi = 1 - x_hi if xi & 2 else x_hi
        lo = 1 - x_lo if xi & 1 else x_lo
        return (hi * RING + z, y * 4 + lo * 2 + kd)

    def in_slice(i2, kd):
        lo = 1 - x_lo if i2 & 1 else x_lo
        yy = y
        if i2 & 2:
            yy = yy + 1 - 2 * lax.rem(y, 2)
        if i2 & 4:
            yy = lax.rem(yy + 2, 4)
        return (ctx, yy * 4 + lo * 2 + kd)

    def remote(src, dst, send, recv, device):
        return pltpu.make_async_remote_copy(
            src_ref=src, dst_ref=dst, send_sem=send, recv_sem=recv, device_id=device, device_id_type=MESH
        )

    first = pl.multiple_of(x_lo * ROWS + core * PIECE, 16)
    column = pl.multiple_of(y * HD, HD)
    own_k = pltpu.make_async_copy(
        k_in.at[pl.ds(first, PIECE), pl.ds(column, HD)], kv.at[core, 0, :, pl.ds(0, HD)], load_sem.at[0]
    )
    own_v = pltpu.make_async_copy(
        v_in.at[pl.ds(first, PIECE), pl.ds(column, HD)], kv.at[core, 0, :, pl.ds(HD, HD)], load_sem.at[1]
    )
    own_q = pltpu.make_async_copy(
        q_in.at[pl.ds(pl.multiple_of(core * ROWS, 16), ROWS)], q.at[0, core], load_sem.at[2]
    )
    own_w = pltpu.make_async_copy(w_in, w.at[core], load_sem.at[3])
    barrier = pltpu.get_barrier_semaphore()
    peers = [along_z(step) for step in (4, -4, 3, -3, 2, -2, 1, -1)]
    peers += [along_x(xi, kd) for xi in (2, 3) for kd in (core, other)]
    peers += [in_slice(i2, kd) for i2 in range(8) for kd in (core, other) if (i2, kd is core) != (0, True)]
    for peer in peers:
        pl.semaphore_signal(barrier, inc=1, device_id=peer, device_id_type=MESH)
    own_k.start()
    own_v.start()
    own_q.start()
    own_w.start()
    acc[...] = jnp.zeros_like(acc)
    row = lax.broadcasted_iota(jnp.int32, stats.shape, 1)
    stats[...] = jnp.where(row == 0, FLOOR, 0.0).astype(jnp.float32)
    own_k.wait()
    own_v.wait()
    pl.semaphore_wait(barrier, len(peers))

    waiting = []

    def z_copy(slot, step, chunk):
        place = PLACE[chunk]
        return remote(
            kv.at[core, PLACE[(0, slot)]], kv.at[core, place], z_send.at[place], z_recv.at[place], along_z(step)
        )

    def pass_on(slot):
        for step, chunk in CHAIN.get(slot, []) + near(slot):
            copy = z_copy(slot, step, chunk)
            copy.start()
            waiting.append(copy)

    def arrived(chunk):
        place = PLACE[chunk]
        remote(
            kv.at[core, place], kv.at[core, place], z_send.at[place], z_recv.at[place], along_z(4)
        ).wait_recv()

    pass_on(0)

    q_copies = []
    for xi in (2, 3, 1, 0):
        for same in (True, False):
            if (xi, same) == (0, True):
                continue
            kd = core if same else other
            copy = remote(
                q_in.at[pl.ds(pl.multiple_of(kd * ROWS, 16), ROWS)],
                q.at[xi, core],
                q_send.at[xi, int(same)],
                q_recv.at[xi, int(same)],
                along_x(xi, kd),
            )
            copy.start()
            q_copies.append((xi, same, copy))
            waiting.append(copy)
    w_copy = remote(w_in, w.at[core], w_send, w_recv, in_slice(0, other))
    w_copy.start()
    waiting.append(w_copy)

    def exchange(wave):
        begin, count = PLACE[WAVES[wave][0]], len(WAVES[wave])
        piece = kv.at[core, pl.ds(begin, count)]
        copy = remote(piece, piece, pair_send.at[wave], pair_recv.at[wave], in_slice(0, other))
        copy.start()
        waiting.append(copy)

    def exchanged(wave):
        begin, count = PLACE[WAVES[wave][0]], len(WAVES[wave])
        theirs = kv.at[other, pl.ds(begin, count)]
        remote(theirs, theirs, pair_send.at[wave], pair_recv.at[wave], in_slice(0, other)).wait_recv()

    def attend(wave, xi, masked):
        begin, count = PLACE[WAVES[wave][0]], len(WAVES[wave])
        queries = jnp.concatenate(
            [q[xi, ks, :, e * HD : (e + 1) * HD] for ks in range(2) for e in range(2)], axis=0
        )
        scores, values = [], []
        for half in range(2):
            block = kv[half, begin : begin + count].reshape(count * PIECE, 2 * HD)
            s = lax.dot_general(
                block[:, :HD], queries, (((1,), (1,)), ((), ())), preferred_element_type=jnp.float32
            )
            if masked:
                pieces = []
                for n in range(count):
                    part = s[n * PIECE : (n + 1) * PIECE]
                    shift = SHIFT[begin + n]
                    if shift == 0:
                        key = lax.broadcasted_iota(jnp.int32, part.shape, 0) + (x_lo * ROWS + half * PIECE)
                        query = lax.rem(lax.broadcasted_iota(jnp.int32, part.shape, 1), ROWS) + core * ROWS
                        pieces.append(jnp.where(key <= query, part, MASKED))
                    else:
                        allowed = lax.rem(z + shift, RING) < z
                        pieces.append(part + jnp.where(allowed, 0.0, MASKED).astype(jnp.float32))
                s = jnp.concatenate(pieces, axis=0)
            scores.append(s)
            values.append(block[:, HD:])
        old = stats[xi, 0:1, :]
        top = old
        for s in scores:
            top = jnp.maximum(top, jnp.max(s, axis=0, keepdims=True))
        factor = jnp.exp2((old - top) * EXP2)
        total = stats[xi, 1:2, :] * factor
        result = acc[xi] * factor
        for s, v in zip(scores, values):
            p = jnp.exp2((s - top) * EXP2)
            total += jnp.sum(p, axis=0, keepdims=True)
            result += lax.dot_general(
                v, p.astype(jnp.bfloat16), (((0,), (0,)), ((), ())), preferred_element_type=jnp.float32
            )
        acc[xi] = result
        stats[xi, 0:1, :] = top
        stats[xi, 1:2, :] = total

    def attend_all(wave):
        @pl.when(x_hi == 0)
        def _():
            @pl.loop(2, 4)
            def _(xi):
                attend(wave, xi, False)

        reached = wave == 0
        for place in range(PLACE[WAVES[wave][0]], PLACE[WAVES[wave][0]] + len(WAVES[wave])):
            if SHIFT[place]:
                reached |= lax.rem(z + SHIFT[place], RING) < z

        @pl.when(reached)
        def _():
            @pl.loop(0, 2)
            def _(xi):
                attend(wave, xi, True)

    def collect(wave):
        for chunk in WAVES[wave]:
            if chunk[0] or chunk[1] == 4:
                arrived(chunk)
        exchange(wave)

    def use(wave):
        exchanged(wave)
        if wave == 0:
            own_q.wait()
            for xi, same, copy in q_copies:
                ks = core if same else other
                remote(
                    q.at[xi, ks], q.at[xi, ks], q_send.at[xi, int(same)], q_recv.at[xi, int(same)], along_x(xi, ks)
                ).wait_recv()
        attend_all(wave)

    for wave in range(len(WAVES)):
        if wave + 1 < len(WAVES):
            for chunk in WAVES[wave + 1]:
                if chunk[0] == 0 and chunk[1] != 4:
                    arrived(chunk)
                    if chunk[1] in (5, 3):
                        continue
                    pass_on(chunk[1])
            if wave == 2:
                last = remote(
                    kv.at[core, PLACE[(0, 3)] + other],
                    kv.at[core, PLACE[(0, 4)]],
                    last_send,
                    z_recv.at[PLACE[(0, 4)]],
                    (x_hi * RING + lax.rem(z + 4 - 8 * core + RING, RING), head),
                )
                last.start()
                waiting.append(last)
                pass_on(3)
                pass_on(5)
        if wave >= 1:
            collect(wave - 1)
        if wave >= 2:
            use(wave - 2)
    collect(len(WAVES) - 1)
    use(len(WAVES) - 2)
    use(len(WAVES) - 1)

    def give(xi, wanted):
        @pl.when(wanted)
        def _():
            sent[xi] = acc[xi].astype(jnp.bfloat16)

        return [
            remote(sent.at[xi], got.at[xi], merge_send.at[xi, 0], merge_recv.at[xi, 0], along_x(xi, core)),
            remote(stats.at[xi], got_stats.at[xi], merge_send.at[xi, 1], merge_recv.at[xi, 1], along_x(xi, core)),
        ]

    def take(xi):
        return [
            remote(got.at[xi], got.at[xi], merge_send.at[xi, 0], merge_recv.at[xi, 0], along_x(xi, core)),
            remote(got_stats.at[xi], got_stats.at[xi], merge_send.at[xi, 1], merge_recv.at[xi, 1], along_x(xi, core)),
        ]

    from_low = [copy for xi in (2, 3) for copy in give(xi, x_hi == 0)]
    pl.when(x_hi == 0)(lambda: [copy.start() for copy in from_low] and None)
    for copy in give(1, True):
        copy.start()
        waiting.append(copy)

    def absorb(xi):
        for copy in take(xi):
            copy.wait_recv()
        mine, theirs = stats[0, 0:1, :], got_stats[xi, 0:1, :]
        top = jnp.maximum(mine, theirs)
        mine, theirs = jnp.exp2((mine - top) * EXP2), jnp.exp2((theirs - top) * EXP2)
        acc[0] = acc[0] * mine + got[xi].astype(jnp.float32) * theirs
        stats[0, 1:2, :] = stats[0, 1:2, :] * mine + got_stats[xi, 1:2, :] * theirs
        stats[0, 0:1, :] = top

    absorb(1)

    @pl.when(x_hi == 1)
    def _():
        absorb(3)
        absorb(2)

    turned = jnp.transpose(acc[0] / stats[0, 1:2, :]).astype(jnp.bfloat16)
    attended = jnp.concatenate([turned[n * ROWS : (n + 1) * ROWS] for n in range(4)], axis=1)

    own_w.wait()
    remote(w_in, w.at[other], w_send, w_recv, in_slice(0, other)).wait_recv()
    for i2 in (6, 7, 4, 5, 2, 3, 1, 0):
        chip = in_slice(i2, 0)[1]
        columns = pl.ds(pl.multiple_of(chip * HD, 2 * HD), 2 * HD)
        sums = jnp.dot(attended[:, : 2 * HD], w[0, :, columns], preferred_element_type=jnp.float32)
        sums += jnp.dot(attended[:, 2 * HD :], w[1, :, columns], preferred_element_type=jnp.float32)
        for kd in range(2):
            parts[i2, kd] = sums[:, kd * HD : (kd + 1) * HD].astype(jnp.bfloat16)
        if i2:
            for kd in range(2):
                copy = remote(
                    parts.at[i2, kd],
                    landed.at[i2, core],
                    sum_send.at[i2, kd],
                    sum_recv.at[i2, core],
                    in_slice(i2, kd),
                )
                copy.start()
                waiting.append(copy)
        else:
            copy = remote(
                parts.at[0, other],
                landed.at[0, core],
                sum_send.at[0, 0],
                sum_recv.at[0, core],
                in_slice(0, other),
            )
            copy.start()
            waiting.append(copy)
    keep = pltpu.make_async_copy(parts.at[0, core], landed.at[0, core], load_sem.at[4])
    keep.start()
    for i2 in range(8):
        for ks in range(2) if i2 else (other,):
            remote(
                landed.at[i2, ks], landed.at[i2, ks], sum_send.at[i2, 0], sum_recv.at[i2, ks], in_slice(i2, other)
            ).wait_recv()
    keep.wait()
    for copy in waiting:
        copy.wait_send()
    pl.when(x_hi == 0)(lambda: [copy.wait_send() for copy in from_low] and None)


def on_device(query_rows, key_rows, value_rows, w_out):
    bf16, f32 = jnp.bfloat16, jnp.float32
    dma = pltpu.SemaphoreType.DMA
    chunks = len(ORDER)
    landed = pl.pallas_call(
        kernel,
        out_shape=jax.ShapeDtypeStruct((8, 2, ROWS, HD), bf16),
        in_specs=[pl.BlockSpec(memory_space=pl.ANY)] * 4,
        out_specs=pl.BlockSpec(memory_space=pl.ANY),
        scratch_shapes=[
            pltpu.VMEM((2, chunks, PIECE, 2 * HD), bf16),
            pltpu.VMEM((4, 2, ROWS, 2 * HD), bf16),
            pltpu.VMEM((2,) + w_out.shape, bf16),
            pltpu.VMEM((4, HD, COLS), f32),
            pltpu.VMEM((4, 8, COLS), f32),
            pltpu.VMEM((4, HD, COLS), bf16),
            pltpu.VMEM((4, HD, COLS), bf16),
            pltpu.VMEM((4, 8, COLS), f32),
            pltpu.VMEM((8, 2, ROWS, HD), bf16),
            dma((5,)),
            dma((chunks,)),
            dma((chunks,)),
            dma,
            dma((len(WAVES),)),
            dma((len(WAVES),)),
            dma((4, 2)),
            dma((4, 2)),
            dma,
            dma,
            dma((4, 2)),
            dma((4, 2)),
            dma((8, 2)),
            dma((8, 2)),
        ],
        compiler_params=pltpu.CompilerParams(
            collective_id=0, has_side_effects=True, vmem_limit_bytes=56 * 1024 * 1024
        ),
        name="attention",
    )(query_rows, key_rows, value_rows, w_out)
    return jnp.sum(landed.astype(f32), axis=0).astype(bf16).reshape(TOK, HD)


def solution(mesh):
    placed = (P("ctx", "head"), P("ctx", None), P("ctx", None), P("head", None))
    return jax.shard_map(
        on_device, mesh=mesh, in_specs=placed, out_specs=P("ctx", "head"), check_vma=False
    )
```
